256 devices in a mesh: seq: 128 (over z, y, x), ch: 2 (over core).
Axes of the slice: x: 4, y: 4, z: 8, core: 2. Of those that a mesh axis runs over, the one named last changes fastest.
Arguments:
- conv_in: bfloat16 [32768, 4096], P('seq', 'ch'), may hold values from -6 to 6
- norm_gain: float32 [4096], P('ch'), may hold values from 0.25 to 1.75
- filters: bfloat16 [256, 128], P('ch'), may hold values from -0.5 to 0.5
- gate: bfloat16 [32768, 4096], P('seq', 'ch'), may hold values from -6 to 6
- queries: bfloat16 [32768, 4096], P('seq', 'ch'), may hold values from -90 to 90
- keys: bfloat16 [32768, 4096], P('seq', 'ch'), may hold values from -6 to 6
- doc_lengths: int32 [48], replicated, may hold values from 1 to 768, 32768 in all
Outputs:
- mixed: bfloat16 [32768, 4096], P('seq', 'ch')
- attended: bfloat16 [32768, 4096], P('seq', 'ch')
The draws below stay inside these ranges and needn't reach their ends.
Inputs may be any that keep to these rules, and one draw needn't show every extreme that they name: `doc_lengths`: no document is longer than 768 tokens, and one has exactly that many; the lengths sum to 32768.
All inputs are finite; a program needn't handle non-finite values.
Results may differ from the reference program's by a relative error of at most 0.0065.
Values may be sent and summed in bfloat16 or wider, within the bound.
No kernel may reach another device: no remote copies, remote signals or barrier semaphores. Data moves between devices by JAX's collectives and lax.ppermute only.
A program may use at most 128 MiB of HBM per device.

```python
import math
import jax
import jax.numpy as jnp
import numpy as np
from jax import lax

HEADS = 32
HEAD_DIM = 128
GROUP = 16
TAPS = 128
SPAN = 4
DOCS = 48
TOK_DEV = 256
CONV_CH = 4096
TOKENS = 32768
MOST_DOC = 768
N_SEQ = 128


def key_base(key):
    return jnp.clip(jax.random.normal(key, (TOKENS, HEADS * HEAD_DIM), jnp.float32), -6.0, 6.0)


def draw_keys(key, part):
    base = key_base(key)
    return base.astype(jnp.bfloat16)


def draw_queries(key, part):
    key = jax.random.fold_in(key, 12)
    fresh = jnp.clip(jax.random.normal(key, (TOKENS, HEADS * HEAD_DIM), jnp.float32), -6.0, 6.0)
    return fresh.astype(jnp.bfloat16)


def steps_of(key, dims, cuts, low, high):
    loudness = 1.0
    for axis_at, shards_of in cuts:
        steps = jax.random.uniform(jax.random.fold_in(jax.random.fold_in(key, 6), axis_at), (shards_of,), jnp.float32, low / len(cuts), high / len(cuts))
        loudness = loudness * jnp.repeat(jnp.exp(steps), dims[axis_at] // shards_of).reshape((-1,) + (1,) * (len(dims) - 1 - axis_at))
    return loudness


def split_up(count, total, bound, slope):
    portions = [(1 << 20) // math.isqrt(standing ** slope) + 1 for standing in range(2, count + 1)]
    spare, holding = total - bound - (count - 1), [1] * (count - 1)
    while spare > 0:
        free = [i for i in range(count - 1) if holding[i] < bound]
        mass, remaining = sum([portions[i] for i in free]), spare
        for i in free:
            addition = min(bound - holding[i], max(1, remaining * portions[i] // mass), spare)
            holding[i] = holding[i] + addition
            spare = spare - addition
    return np.array([bound] + holding)


def ragged(stream_key, amount, total, limit, skew):
    if amount == 2:
        one = jax.random.randint(stream_key, (), max(1, total - limit), min(limit, total - 1) + 1)
        return jnp.stack([one, total - one])
    lengths = jnp.asarray(split_up(amount, total, limit, skew), jnp.int32)
    pairs = (amount - 1) // 2
    donor, receiver = lengths[1:1 + 2 * pairs:2], lengths[2:2 + 2 * pairs:2]
    slack = jnp.minimum(donor - 1, limit - receiver)
    moved = jax.random.randint(jax.random.fold_in(stream_key, 1), (pairs,), 0, 1 << 20) % (slack + 1)
    lengths = lengths.at[1:1 + 2 * pairs:2].set(donor - moved).at[2:2 + 2 * pairs:2].set(receiver + moved)
    return lengths[jax.random.permutation(jax.random.fold_in(stream_key, 2), amount)]


def noise(stream_key, dims, scale, bound, shards=(), kind=jnp.bfloat16):
    factor_of = steps_of(stream_key, dims, shards, -0.22, 0.18) if shards else 1.0
    array = jax.random.normal(stream_key, dims, jnp.float32) * scale * factor_of
    return jnp.minimum(jnp.maximum(array, -bound), bound).astype(kind)


def setup_inputs(seed: int = 0) -> dict:
    key_of = jax.random.split(jax.random.key(seed), 8)
    return {
        "conv_in": noise(key_of[0], (TOKENS, CONV_CH), 1.0, 6.0, ((0, 128), (1, 2))),
        "norm_gain": jnp.clip(1.0 + 0.15 * jax.random.normal(key_of[1], (CONV_CH,), jnp.float32), 0.25, 1.75),
        "filters": noise(key_of[2], (CONV_CH // GROUP, TAPS), TAPS ** -0.5, 0.5, ((0, 2),)),
        "gate": noise(key_of[3], (TOKENS, CONV_CH), 1.0, 6.0, ((0, 128), (1, 2))),
        "queries": draw_queries(jax.random.fold_in(key_of[7], 71), 0),
        "keys": draw_keys(jax.random.fold_in(key_of[7], 71), 0),
        "doc_lengths": ragged(key_of[6], DOCS, TOKENS, MOST_DOC, 2).astype(jnp.int32),
    }


def begin_of(doc_lengths, positions):
    ends = jnp.cumsum(doc_lengths).astype(jnp.int32)
    starts = ends - doc_lengths
    inside = starts[None, :] <= positions[:, None]
    return lax.optimization_barrier(jnp.max(jnp.where(inside, starts[None, :], 0), axis=1)).astype(jnp.int32)

def toeplitz(filters, out_pos, src_pos, begin):
    taps_count = filters.shape[1]
    lag = out_pos[:, None] - src_pos[None, :]
    valid = (lag >= 0) & (lag < taps_count) & (src_pos[None, :] >= begin[:, None])
    taps = jnp.take(filters, jnp.clip(lag, 0, taps_count - 1), axis=1)
    return jnp.where(valid[None], taps, jnp.zeros_like(taps))

def reference(conv_in, norm_gain, filters, gate, queries, keys, doc_lengths):
    positions = jnp.arange(TOKENS, dtype=jnp.int32)
    begin = begin_of(doc_lengths, positions)
    wide = conv_in.astype(jnp.float32)
    energy = lax.optimization_barrier(jnp.sum(wide * wide, axis=1))
    normed = (wide * lax.rsqrt(energy / CONV_CH + 1e-06)[:, None] * norm_gain[None, :]).astype(jnp.bfloat16)
    padded = jnp.concatenate([jnp.zeros((TAPS, CONV_CH), jnp.bfloat16), normed], axis=0)
    groups = CONV_CH // GROUP

    def conv_block(index):
        start = (index * TAPS).astype(jnp.int32)
        source = lax.dynamic_slice_in_dim(padded, start, 2 * TAPS, 0)
        out_pos = start + jnp.arange(TAPS, dtype=jnp.int32)
        src_pos = start - TAPS + jnp.arange(2 * TAPS, dtype=jnp.int32)
        matrix = toeplitz(filters, out_pos, src_pos, lax.dynamic_slice_in_dim(begin, start, TAPS, 0))
        filt = jnp.einsum('gnm,mgc->ngc', matrix.astype(jnp.float32), source.reshape(2 * TAPS, groups, GROUP).astype(jnp.float32))
        gated = lax.dynamic_slice_in_dim(gate, start, TAPS, 0).astype(jnp.float32)
        return (gated * filt.reshape(TAPS, CONV_CH)).astype(jnp.bfloat16)
    mixed = lax.map(conv_block, jnp.arange(TOKENS // TAPS, dtype=jnp.int32)).reshape(TOKENS, CONV_CH)
    back = (SPAN - 1) * TOK_DEV
    key_pad = jnp.concatenate([jnp.zeros((back, CONV_CH), jnp.bfloat16), keys], axis=0)
    val_pad = jnp.concatenate([jnp.zeros((back, CONV_CH), jnp.bfloat16), mixed], axis=0)
    scale = HEAD_DIM ** (-0.5)

    def attend(index):
        start = (index * TOK_DEV).astype(jnp.int32)
        query = lax.dynamic_slice_in_dim(queries, start, TOK_DEV, 0).reshape(TOK_DEV, HEADS, HEAD_DIM).astype(jnp.float32)
        key_blk = lax.dynamic_slice_in_dim(key_pad, start, SPAN * TOK_DEV, 0).reshape(SPAN * TOK_DEV, HEADS, HEAD_DIM).astype(jnp.float32)
        val_blk = lax.dynamic_slice_in_dim(val_pad, start, SPAN * TOK_DEV, 0).reshape(SPAN * TOK_DEV, HEADS, HEAD_DIM).astype(jnp.float32)
        qpos = start + jnp.arange(TOK_DEV, dtype=jnp.int32)
        kpos = start - back + jnp.arange(SPAN * TOK_DEV, dtype=jnp.int32)
        first = lax.dynamic_slice_in_dim(begin, start, TOK_DEV, 0)
        valid = (kpos[None, :] <= qpos[:, None]) & (kpos[None, :] >= first[:, None])
        score = jnp.einsum('rhd,khd->hrk', query, key_blk) * scale
        score = jnp.where(valid[None], score, -1e+30)
        top = lax.optimization_barrier(jnp.max(score, axis=2, keepdims=True))
        weight = jnp.where(valid[None], jnp.exp(score - top), 0.0)
        total = lax.optimization_barrier(jnp.sum(weight, axis=2))
        rounded = lax.optimization_barrier(weight.astype(jnp.bfloat16)).astype(jnp.float32)
        output = jnp.einsum('hrk,khd->rhd', rounded, val_blk) / total.T[:, :, None]
        return output.astype(jnp.bfloat16).reshape(TOK_DEV, CONV_CH)
    attended = lax.map(attend, jnp.arange(N_SEQ, dtype=jnp.int32)).reshape(TOKENS, CONV_CH)
    return (mixed, attended)
```

```python
import jax
import jax.numpy as jnp
from jax import lax
from jax.experimental import pallas as pl
from jax.experimental.pallas import tpu as pltpu
from jax.sharding import PartitionSpec as P

HEAD_DIM = 128
GROUP = 16
TAPS = 128
CONV_CH = 4096
RING = 4
VMEM_LIMIT = 48 * 1024 * 1024
ANY = pl.BlockSpec(memory_space=pl.ANY)
SMEM = pl.BlockSpec(memory_space=pltpu.SMEM)
VMEM = pl.BlockSpec(memory_space=pltpu.VMEM)
NEG = -1e30


def begin_of(doc_lengths, positions):
    ends = jnp.cumsum(doc_lengths)
    starts = ends - doc_lengths
    inside = starts[None, :] <= positions[:, None]
    return jnp.max(jnp.where(inside, starts[None, :], 0), axis=1)


def params():
    return pltpu.CompilerParams(vmem_limit_bytes=VMEM_LIMIT)


def cost(flops, nbytes, trans=0):
    return pl.CostEstimate(flops=flops, bytes_accessed=nbytes, transcendentals=trans)


def quarters(place, *arrays):
    rows, width = arrays[0].shape
    part = width // RING
    count = len(arrays)

    def kernel(place_ref, *refs):
        ins, outs, sem = refs[:count], refs[count : count + count * RING], refs[-1]
        place = place_ref[0]
        copies = []
        for a in range(count):
            for d in range(RING):
                low = pl.multiple_of(lax.rem(place + d, RING) * part, part)
                copies.append(
                    pltpu.make_async_copy(
                        ins[a].at[:, pl.ds(low, part)], outs[a * RING + d], sem.at[a * RING + d]
                    )
                )
        for copy in copies:
            copy.start()
        for copy in copies:
            copy.wait()

    out = pl.pallas_call(
        kernel,
        out_shape=[
            jax.ShapeDtypeStruct((rows, part), arrays[0].dtype) for _ in range(count * RING)
        ],
        in_specs=[SMEM] + [ANY] * count,
        out_specs=[ANY] * (count * RING),
        scratch_shapes=[pltpu.SemaphoreType.DMA((count * RING,))],
        compiler_params=params(),
        cost_estimate=cost(0, 4 * count * rows * width),
        name="quarters",
    )(place, *arrays)
    return [out[a * RING : (a + 1) * RING] for a in range(count)]


def whole_width(place, pieces):
    rows, part = pieces[0].shape

    def kernel(place_ref, *refs):
        ins, out, sem = refs[:RING], refs[RING], refs[-1]
        place = place_ref[0]
        copies = []
        for d in range(RING):
            low = pl.multiple_of(lax.rem(place + RING - d, RING) * part, part)
            copies.append(
                pltpu.make_async_copy(ins[d], out.at[:, pl.ds(low, part)], sem.at[d])
            )
        for copy in copies:
            copy.start()
        for copy in copies:
            copy.wait()

    return pl.pallas_call(
        kernel,
        out_shape=jax.ShapeDtypeStruct((rows, part * RING), pieces[0].dtype),
        in_specs=[SMEM] + [ANY] * RING,
        out_specs=ANY,
        scratch_shapes=[pltpu.SemaphoreType.DMA((RING,))],
        compiler_params=params(),
        cost_estimate=cost(0, 4 * rows * part * RING),
        name="whole_width",
    )(place, *pieces)


def last_shards(place, pieces):
    rows, part = pieces[0].shape

    def kernel(place_ref, *refs):
        ins, out, sem = refs[:RING], refs[RING], refs[-1]
        place = place_ref[0]

        def copy_of(d):
            shard = lax.rem(place + RING - d, RING)
            low = pl.multiple_of(jnp.maximum(shard - 1, 0) * rows, rows)
            return shard, pltpu.make_async_copy(ins[d], out.at[pl.ds(low, rows), :], sem.at[d])

        for d in range(RING):
            shard, copy = copy_of(d)
            pl.when(shard > 0)(copy.start)
        for d in range(RING):
            shard, copy = copy_of(d)
            pl.when(shard > 0)(copy.wait)

    return pl.pallas_call(
        kernel,
        out_shape=jax.ShapeDtypeStruct((rows * (RING - 1), part), pieces[0].dtype),
        in_specs=[SMEM] + [ANY] * RING,
        out_specs=ANY,
        scratch_shapes=[pltpu.SemaphoreType.DMA((RING,))],
        compiler_params=params(),
        cost_estimate=cost(0, 3 * rows * part * RING),
        name="last_shards",
    )(place, *pieces)


def convolve(place, conv_in, tail, rms, gain, taps, gate, begin):
    rows, width = conv_in.shape
    part = width // RING
    lanes = 128
    per = lanes // GROUP
    blocks = rows // TAPS

    def kernel(place_ref, x_ref, tail_ref, rms_ref, gain_ref, taps_ref, gate_ref, begin_ref, *refs):
        mixed_ref, outs = refs[0], refs[1 : 1 + RING]
        masks, src, lhs = refs[1 + RING :]
        place = place_ref[0]
        out_row = lax.broadcasted_iota(jnp.int32, (TAPS, lanes), 0)
        src_col = lax.broadcasted_iota(jnp.int32, (TAPS, lanes), 1)
        for b in range(blocks):
            first = begin_ref[b * TAPS : (b + 1) * TAPS, :]
            low = b * TAPS
            before = (src_col > out_row) & (src_col + (low - TAPS) >= first)
            inside = (src_col <= out_row) & (src_col + low >= first)
            masks[2 * b] = jnp.where(before, 1.0, 0.0).astype(jnp.bfloat16)
            masks[2 * b + 1] = jnp.where(inside, 1.0, 0.0).astype(jnp.bfloat16)
        lane_group = lax.broadcasted_iota(jnp.int32, (TAPS, lanes), 1) // GROUP

        def chunk(d, c):
            at = lax.rem(place + d, RING) * (part // lanes) + c
            low = pl.multiple_of(at * lanes, lanes)
            cols = pl.ds(low, lanes)
            src[:TAPS, :] = tail_ref[:, cols]
            src[TAPS:, :] = (
                x_ref[:, cols].astype(jnp.float32) * rms_ref[...] * gain_ref[:, cols]
            ).astype(jnp.bfloat16)
            rows8 = taps_ref[pl.ds(pl.multiple_of(at * per, per), per), :]
            for j in range(per):
                line = jnp.broadcast_to(rows8[j : j + 1, :], (TAPS, lanes))
                band = pltpu.roll(line, 1, 1, stride=1, stride_axis=0).astype(jnp.bfloat16)
                for b in range(blocks):
                    at_rows = pl.ds(j * TAPS, TAPS)
                    lhs[b, at_rows, :lanes] = band * masks[2 * b]
                    lhs[b, at_rows, lanes:] = band * masks[2 * b + 1]
            for b in range(blocks):
                full = jnp.dot(
                    lhs[b],
                    src[b * TAPS : (b + 2) * TAPS, :],
                    preferred_element_type=jnp.float32,
                )
                picked = full[:TAPS]
                for j in range(1, per):
                    picked = jnp.where(lane_group == j, full[j * TAPS : (j + 1) * TAPS], picked)
                at_rows = pl.ds(b * TAPS, TAPS)
                out = (gate_ref[at_rows, cols].astype(jnp.float32) * picked).astype(jnp.bfloat16)
                mixed_ref[at_rows, cols] = out
                outs[d][at_rows, c * lanes : (c + 1) * lanes] = out

        for d in (2, 1, 3, 0):
            for c in range(part // lanes):
                chunk(d, c)

    out = pl.pallas_call(
        kernel,
        out_shape=[jax.ShapeDtypeStruct((rows, width), jnp.bfloat16)]
        + [jax.ShapeDtypeStruct((rows, part), jnp.bfloat16) for _ in range(RING)],
        in_specs=[SMEM] + [VMEM] * 7,
        out_specs=[VMEM] * (1 + RING),
        scratch_shapes=[
            pltpu.VMEM((2 * blocks, TAPS, lanes), jnp.bfloat16),
            pltpu.VMEM((rows + TAPS, lanes), jnp.bfloat16),
            pltpu.VMEM((blocks, per * TAPS, 2 * lanes), jnp.bfloat16),
        ],
        compiler_params=params(),
        cost_estimate=cost(2 * rows * 2 * TAPS * width * per, 10 * rows * width),
        name="convolve",
    )(place, conv_in, tail, rms, gain, taps, gate, begin)
    return out[0], list(out[1:])


def attend(place, begin, queries, keys, values, key_halo, value_halo):
    rows, part = queries[0].shape
    heads = part // HEAD_DIM
    back = (RING - 1) * rows
    span = RING * rows
    scale = HEAD_DIM**-0.5 * 1.4426950408889634

    def kernel(place_ref, begin_ref, *refs):
        q_in, k_in, v_in = refs[:RING], refs[RING : 2 * RING], refs[2 * RING : 3 * RING]
        kh_in, vh_in = refs[3 * RING : 3 * RING + 2]
        outs = refs[3 * RING + 2 : 4 * RING + 2]
        q_all, k_all, v_all, o_all, bias, sem, out_sem = refs[4 * RING + 2 :]
        place = place_ref[0]
        copies = []

        def fetch(source, target):
            copies.append(pltpu.make_async_copy(source, target, sem.at[len(copies)]))

        for d in range(RING):
            low = pl.multiple_of(lax.rem(place + RING - d, RING) * rows, rows)
            fetch(q_in[d], q_all.at[pl.ds(low, rows), :])
            fetch(k_in[d], k_all.at[pl.ds(back + low, rows), :])
            fetch(v_in[d], v_all.at[pl.ds(back + low, rows), :])
        fetch(kh_in, k_all.at[pl.ds(0, back), :])
        fetch(vh_in, v_all.at[pl.ds(0, back), :])
        for copy in copies:
            copy.start()
        for copy in copies:
            copy.wait()
        row = lax.broadcasted_iota(jnp.int32, (rows, 128), 0)
        col = lax.broadcasted_iota(jnp.int32, (rows, 128), 1)

        def shard(s, _):
            low = pl.multiple_of(s * rows, rows)
            first = begin_ref[pl.ds(low, rows), :] - low
            for c in range(span // 128):
                key = col + c * 128
                valid = key >= first
                if (c + 1) * 128 > back:
                    valid = valid & (key <= row + back)
                bias[:, c * 128 : (c + 1) * 128] = jnp.where(valid, 0.0, NEG)
            for h in range(heads):
                cols = slice(h * HEAD_DIM, (h + 1) * HEAD_DIM)
                score = lax.dot_general(
                    q_all[pl.ds(low, rows), cols],
                    k_all[pl.ds(low, span), cols],
                    (((1,), (1,)), ((), ())),
                    preferred_element_type=jnp.float32,
                )
                score = score + bias[...]
                top = jnp.max(score, axis=1, keepdims=True)
                weight = jnp.exp2((score - top) * scale)
                total = jnp.sum(weight, axis=1, keepdims=True)
                acc = jnp.dot(
                    weight.astype(jnp.bfloat16),
                    v_all[pl.ds(low, span), cols],
                    preferred_element_type=jnp.float32,
                )
                o_all[pl.ds(low, rows), cols] = (acc / total).astype(jnp.bfloat16)
            return 0

        lax.fori_loop(0, RING, shard, 0)
        sends = []
        for d in range(RING):
            low = pl.multiple_of(lax.rem(place + d, RING) * rows, rows)
            sends.append(
                pltpu.make_async_copy(o_all.at[pl.ds(low, rows), :], outs[d], out_sem.at[d])
            )
        for send in sends:
            send.start()
        for send in sends:
            send.wait()

    return pl.pallas_call(
        kernel,
        out_shape=[jax.ShapeDtypeStruct((rows, part), jnp.bfloat16) for _ in range(RING)],
        in_specs=[SMEM, VMEM] + [ANY] * (3 * RING + 2),
        out_specs=[ANY] * RING,
        scratch_shapes=[
            pltpu.VMEM((span, part), jnp.bfloat16),
            pltpu.VMEM((back + span, part), jnp.bfloat16),
            pltpu.VMEM((back + span, part), jnp.bfloat16),
            pltpu.VMEM((span, part), jnp.bfloat16),
            pltpu.VMEM((rows, span), jnp.float32),
            pltpu.SemaphoreType.DMA((3 * RING + 2,)),
            pltpu.SemaphoreType.DMA((RING,)),
        ],
        compiler_params=params(),
        cost_estimate=cost(
            16 * RING * heads * rows * span * HEAD_DIM, 16 * rows * part * RING, heads * span * span
        ),
        name="attend",
    )(place, begin, *queries, *keys, *values, key_halo, value_halo)


def shards(conv_in, norm_gain, filters, gate, queries, keys, doc_lengths):
    rows, width = conv_in.shape
    count = lax.axis_size("seq")
    index = lax.axis_index("seq")
    base = index * rows
    place = lax.rem(index, RING)
    ring_base = (index - place) * rows
    place = place.reshape(1)

    def ring_perm(value, step):
        pairs = [
            (r + i, r + (i + step) % RING) for r in range(0, count, RING) for i in range(RING)
        ]
        return lax.ppermute(value, "seq", pairs)

    def exchange(pieces):
        return [pieces[0]] + [ring_perm(pieces[d], d) for d in range(1, RING)]

    def ahead(value, step):
        return lax.ppermute(value, "seq", [(i, i + step) for i in range(count - step)])

    (query_out, key_out) = quarters(place, queries, keys)
    key_in = exchange(key_out)

    wide = conv_in.astype(jnp.float32)
    energy = lax.psum(jnp.sum(wide * wide, axis=1), "ch")
    rms = lax.rsqrt(energy / CONV_CH + 1e-06)
    rms_wide = jnp.broadcast_to(rms[:, None], (rows, 128))
    last = (
        conv_in[rows - TAPS :].astype(jnp.float32)
        * rms[rows - TAPS :, None]
        * norm_gain[None, :]
    ).astype(jnp.bfloat16)
    tail = ahead(last, 1)

    positions = ring_base + jnp.arange(rows * RING, dtype=jnp.int32)
    begin_ring = begin_of(doc_lengths, positions)
    begin_att = jnp.broadcast_to(
        (begin_ring - ring_base + (RING - 1) * rows)[:, None], (rows * RING, 128)
    )
    begin_own = begin_of(doc_lengths, base + jnp.arange(rows, dtype=jnp.int32)) - base
    begin_conv = jnp.broadcast_to(begin_own[:, None], (rows, 128))

    taps = filters[:, ::-1].astype(jnp.float32)
    mixed, value_out = convolve(
        place, conv_in, tail, rms_wide, norm_gain[None, :], taps, gate, begin_conv
    )
    query_in = exchange(query_out)
    value_in = exchange(value_out)
    key_halo = ahead(last_shards(place, key_in), RING)
    value_halo = ahead(last_shards(place, value_in), RING)
    pieces = attend(place, begin_att, query_in, key_in, value_in, key_halo, value_halo)
    attended = whole_width(place, exchange(pieces))
    return (mixed, attended)


def solution(mesh):
    placed = (
        P("seq", "ch"),
        P("ch"),
        P("ch", None),
        P("seq", "ch"),
        P("seq", "ch"),
        P("seq", "ch"),
        P(),
    )
    return jax.shard_map(
        shards,
        mesh=mesh,
        in_specs=placed,
        out_specs=(P("seq", "ch"), P("seq", "ch")),
        check_vma=False,
    )
```

```python
import jax
import jax.numpy as jnp
from jax import lax
from jax.experimental import pallas as pl
from jax.experimental.pallas import tpu as pltpu
from jax.sharding import PartitionSpec as P

HEAD_DIM = 128
GROUP = 16
TAPS = 128
CONV_CH = 4096
RING = 4
CUTS = 1
MIB = 1024 * 1024
HBM = pl.BlockSpec(memory_space=pltpu.HBM)
SMEM = pl.BlockSpec(memory_space=pltpu.SMEM)
VMEM = pl.BlockSpec(memory_space=pltpu.VMEM)
NEG = -1e30


def begin_of(doc_lengths, positions):
    ends = jnp.cumsum(doc_lengths)
    starts = ends - doc_lengths
    inside = starts[None, :] <= positions[:, None]
    return jnp.max(jnp.where(inside, starts[None, :], 0), axis=1)


def params(mib):
    return pltpu.CompilerParams(vmem_limit_bytes=mib * MIB)


def quarters(place, *arrays):
    rows, width = arrays[0].shape
    part = width // RING
    count = len(arrays)

    def kernel(place_ref, *refs):
        ins, outs, sem = refs[:count], refs[count : count + count * RING], refs[-1]
        place = place_ref[0]
        copies = []
        for a in range(count):
            for d in range(RING):
                low = pl.multiple_of(lax.rem(place + d, RING) * part, part)
                copies.append(
                    pltpu.make_async_copy(
                        ins[a].at[:, pl.ds(low, part)], outs[a * RING + d], sem.at[a * RING + d]
                    )
                )
        for copy in copies:
            copy.start()
        for copy in copies:
            copy.wait()

    out = pl.pallas_call(
        kernel,
        out_shape=[
            jax.ShapeDtypeStruct((rows, part), arrays[0].dtype) for _ in range(count * RING)
        ],
        in_specs=[SMEM] + [HBM] * count,
        out_specs=[VMEM] * (count * RING),
        scratch_shapes=[pltpu.SemaphoreType.DMA((count * RING,))],
        compiler_params=params(8),
        name="quarters",
    )(place, *arrays)
    return [out[a * RING : (a + 1) * RING] for a in range(count)]


def whole_width(place, sets):
    rows, width = sets[0][0].shape
    cuts = len(sets)

    def kernel(place_ref, *refs):
        ins, out, sem = refs[: RING * cuts], refs[RING * cuts], refs[-1]
        place = place_ref[0]
        copies = []
        for c in range(cuts):
            for d in range(RING):
                at = c * RING + d
                low = (lax.rem(place + RING - d, RING) * cuts + c) * width
                cols = pl.ds(pl.multiple_of(low, width), width)
                copies.append(pltpu.make_async_copy(ins[at], out.at[:, cols], sem.at[at]))
        for copy in copies:
            copy.start()
        for copy in copies:
            copy.wait()

    return pl.pallas_call(
        kernel,
        out_shape=jax.ShapeDtypeStruct((rows, width * cuts * RING), sets[0][0].dtype),
        in_specs=[SMEM] + [VMEM] * (RING * cuts),
        out_specs=HBM,
        scratch_shapes=[pltpu.SemaphoreType.DMA((RING * cuts,))],
        compiler_params=params(8),
        name="whole_width",
    )(place, *[piece for pieces in sets for piece in pieces])


def last_shards(place, pieces, cuts):
    rows, part = pieces[0].shape
    width = part // cuts

    def kernel(place_ref, *refs):
        ins, outs, sem = refs[:RING], refs[RING : RING + cuts], refs[-1]
        place = place_ref[0]

        def copy_of(d, c):
            shard = lax.rem(place + RING - d, RING)
            low = pl.multiple_of(jnp.maximum(shard - 1, 0) * rows, rows)
            return shard, pltpu.make_async_copy(
                ins[d].at[:, pl.ds(c * width, width)],
                outs[c].at[pl.ds(low, rows), :],
                sem.at[d * cuts + c],
            )

        every = [(d, c) for d in range(RING) for c in range(cuts)]
        for d, c in every:
            shard, copy = copy_of(d, c)
            pl.when(shard > 0)(copy.start)
        for d, c in every:
            shard, copy = copy_of(d, c)
            pl.when(shard > 0)(copy.wait)

    return pl.pallas_call(
        kernel,
        out_shape=[
            jax.ShapeDtypeStruct((rows * (RING - 1), width), pieces[0].dtype) for _ in range(cuts)
        ],
        in_specs=[SMEM] + [VMEM] * RING,
        out_specs=[VMEM] * cuts,
        scratch_shapes=[pltpu.SemaphoreType.DMA((RING * cuts,))],
        compiler_params=params(8),
        name="last_shards",
    )(place, *pieces)


def convolve_own(place, conv_in, rms, gain, taps, gate, begin):
    rows, width = conv_in.shape
    lanes = 128
    per = lanes // GROUP
    blocks = rows // TAPS

    def kernel(x_ref, rms_ref, gain_ref, taps_ref, gate_ref, begin_ref, *refs):
        mixed_ref, part_ref, band_ref, masks, src, lhs = refs
        out_row = lax.broadcasted_iota(jnp.int32, (TAPS, lanes), 0)
        src_col = lax.broadcasted_iota(jnp.int32, (TAPS, lanes), 1)
        for b in range(blocks):
            first = begin_ref[b * TAPS : (b + 1) * TAPS, :]
            low = b * TAPS
            before = (src_col > out_row) & (src_col + (low - TAPS) >= first)
            inside = (src_col <= out_row) & (src_col + low >= first)
            masks[2 * b] = jnp.where(before, 1.0, 0.0).astype(jnp.bfloat16)
            masks[2 * b + 1] = jnp.where(inside, 1.0, 0.0).astype(jnp.bfloat16)
        lane_group = lax.broadcasted_iota(jnp.int32, (TAPS, lanes), 1) // GROUP

        def pick(full):
            picked = full[:TAPS]
            for j in range(1, per):
                picked = jnp.where(lane_group == j, full[j * TAPS : (j + 1) * TAPS], picked)
            return picked

        for at in range(width // lanes):
            cols = slice(at * lanes, (at + 1) * lanes)
            src[...] = (
                x_ref[:, cols].astype(jnp.float32) * rms_ref[...] * gain_ref[:, cols]
            ).astype(jnp.bfloat16)
            for j in range(per):
                line = jnp.broadcast_to(
                    taps_ref[at * per + j : at * per + j + 1, :], (TAPS, lanes)
                )
                band = pltpu.roll(line, 1, 1, stride=1, stride_axis=0).astype(jnp.bfloat16)
                spot = slice(j * TAPS, (j + 1) * TAPS)
                band_ref[at, spot, :] = band * masks[0]
                lhs[0, spot, :lanes] = band * masks[1]
                for b in range(1, blocks):
                    lhs[b, spot, :lanes] = band * masks[2 * b]
                    lhs[b, spot, lanes:] = band * masks[2 * b + 1]
            part_ref[:, cols] = pick(
                jnp.dot(lhs[0, :, :lanes], src[:TAPS, :], preferred_element_type=jnp.float32)
            )
            for b in range(1, blocks):
                full = jnp.dot(
                    lhs[b],
                    src[(b - 1) * TAPS : (b + 1) * TAPS, :],
                    preferred_element_type=jnp.float32,
                )
                here = slice(b * TAPS, (b + 1) * TAPS)
                mixed_ref[(b - 1) * TAPS : b * TAPS, cols] = (
                    gate_ref[here, cols].astype(jnp.float32) * pick(full)
                ).astype(jnp.bfloat16)

    return pl.pallas_call(
        kernel,
        out_shape=[
            jax.ShapeDtypeStruct((rows - TAPS, width), jnp.bfloat16),
            jax.ShapeDtypeStruct((TAPS, width), jnp.float32),
            jax.ShapeDtypeStruct((width // lanes, per * TAPS, lanes), jnp.bfloat16),
        ],
        in_specs=[VMEM] * 6,
        out_specs=[VMEM] * 3,
        scratch_shapes=[
            pltpu.VMEM((2 * blocks, TAPS, lanes), jnp.bfloat16),
            pltpu.VMEM((rows, lanes), jnp.bfloat16),
            pltpu.VMEM((blocks, per * TAPS, 2 * lanes), jnp.bfloat16),
        ],
        compiler_params=params(20),
        name="convolve_own",
    )(conv_in, rms, gain, taps, gate, begin)


def convolve_tail(place, tail, part, bands, rest, gate):
    width = tail.shape[1]
    rows = TAPS + rest.shape[0]
    block = width // RING
    lanes = 128
    per = lanes // GROUP

    def kernel(place_ref, tail_ref, part_ref, band_ref, rest_ref, gate_ref, *refs):
        mixed_ref, outs = refs[0], refs[1:]
        place = place_ref[0]
        lane_group = lax.broadcasted_iota(jnp.int32, (TAPS, lanes), 1) // GROUP
        for d in range(RING):
            for c in range(block // lanes):
                at = lax.rem(place + d, RING) * (block // lanes) + c
                cols = pl.ds(pl.multiple_of(at * lanes, lanes), lanes)
                mine = slice(c * lanes, (c + 1) * lanes)
                full = jnp.dot(band_ref[at], tail_ref[:, cols], preferred_element_type=jnp.float32)
                picked = full[:TAPS]
                for j in range(1, per):
                    picked = jnp.where(lane_group == j, full[j * TAPS : (j + 1) * TAPS], picked)
                out = (
                    gate_ref[:TAPS, cols].astype(jnp.float32) * (part_ref[:, cols] + picked)
                ).astype(jnp.bfloat16)
                mixed_ref[:TAPS, cols] = out
                outs[d][:TAPS, mine] = out
                other = rest_ref[:, cols]
                mixed_ref[TAPS:, cols] = other
                outs[d][TAPS:, mine] = other

    out = pl.pallas_call(
        kernel,
        out_shape=[jax.ShapeDtypeStruct((rows, width), jnp.bfloat16)]
        + [jax.ShapeDtypeStruct((rows, block), jnp.bfloat16) for _ in range(RING)],
        in_specs=[SMEM] + [VMEM] * 5,
        out_specs=[VMEM] * (1 + RING),
        compiler_params=params(16),
        name="convolve_tail",
    )(place, tail, part, bands, rest, gate)
    return out[0], list(out[1:])


SCALE = HEAD_DIM**-0.5 * 1.4426950408889634
BOTH_LAST = (((1,), (1,)), ((), ()))


def attend_ring(place, begin, queries, keys, values):
    rows, part = queries[0].shape
    heads = part // HEAD_DIM
    span = RING * rows

    def kernel(place_ref, begin_ref, *refs):
        ins = (refs[:RING], refs[RING : 2 * RING], refs[2 * RING : 3 * RING])
        acc_ref, top_ref, total_ref, q_all, k_all, v_all, sem = refs[3 * RING :]
        alls = (q_all, k_all, v_all)
        place = place_ref[0]
        for d in range(RING):
            shard = lax.rem(place + RING - d, RING)
            low = pl.multiple_of(shard * rows, rows)
            for a in range(3):
                pltpu.make_async_copy(
                    ins[a][d], alls[a].at[pl.ds(low, rows), :], sem.at[a, shard]
                ).start()
        for s in range(RING):
            here = slice(s * rows, (s + 1) * rows)
            size = (s + 1) * rows
            for a in range(3):
                pltpu.make_async_copy(ins[a][0], alls[a].at[here, :], sem.at[a, s]).wait()
            first = begin_ref[here, :]
            key = lax.broadcasted_iota(jnp.int32, (rows, 128), 1)
            row = lax.broadcasted_iota(jnp.int32, (rows, 128), 0) + s * rows
            bias = []
            for c in range(size // 128):
                valid = key + c * 128 >= first
                if (c + 1) * 128 > s * rows:
                    valid = valid & (key + c * 128 <= row)
                bias.append(jnp.where(valid, 0.0, NEG))
            bias = jnp.concatenate(bias, axis=1)
            for h in range(heads):
                cols = slice(h * HEAD_DIM, (h + 1) * HEAD_DIM)
                score = bias + lax.dot_general(
                    q_all[here, cols],
                    k_all[:size, cols],
                    BOTH_LAST,
                    preferred_element_type=jnp.float32,
                )
                top = jnp.max(score, axis=1, keepdims=True)
                weight = jnp.exp2((score - top) * SCALE)
                total = jnp.sum(weight, axis=1, keepdims=True)
                acc_ref[here, cols] = jnp.dot(
                    weight.astype(jnp.bfloat16),
                    v_all[:size, cols],
                    preferred_element_type=jnp.float32,
                )
                top_ref[here, cols] = jnp.broadcast_to(top, (rows, HEAD_DIM))
                total_ref[here, cols] = jnp.broadcast_to(total, (rows, HEAD_DIM))

    return pl.pallas_call(
        kernel,
        out_shape=[jax.ShapeDtypeStruct((span, part), jnp.float32) for _ in range(3)]
        + [jax.ShapeDtypeStruct((span, part), jnp.bfloat16)],
        in_specs=[SMEM] + [VMEM] * (1 + 3 * RING),
        out_specs=[VMEM] * 4,
        scratch_shapes=[
            pltpu.VMEM((span, part), jnp.bfloat16),
            pltpu.VMEM((span, part), jnp.bfloat16),
            pltpu.SemaphoreType.DMA((3, RING)),
        ],
        compiler_params=params(20),
        name="attend_ring",
    )(place, begin, *queries, *keys, *values)


def attend_halo(place, begin, sums, queries, key_halo, value_halo):
    back, part = value_halo.shape
    rows = back // (RING - 1)
    heads = part // HEAD_DIM
    span = RING * rows

    def kernel(place_ref, begin_ref, acc_ref, top_ref, total_ref, q_ref, k_ref, v_ref, *refs):
        outs, o_all, sem = refs[:RING], refs[RING], refs[RING + 1]
        place = place_ref[0]
        for s in (3, 0, 1, 2):
            here = slice(s * rows, (s + 1) * rows)
            size = (RING - 1 - s) * rows
            low = s * rows
            if size:
                first = begin_ref[here, :]
                key = lax.broadcasted_iota(jnp.int32, (rows, 128), 1) + (low - back)
                bias = jnp.concatenate(
                    [jnp.where(key + c * 128 >= first, 0.0, NEG) for c in range(size // 128)],
                    axis=1,
                )
            for h in range(heads):
                cols = slice(h * HEAD_DIM, (h + 1) * HEAD_DIM)
                top = top_ref[here, cols]
                total = total_ref[here, cols]
                out = acc_ref[here, cols]
                if size:
                    score = bias + lax.dot_general(
                        q_ref[here, cols],
                        k_ref[low:, cols],
                        BOTH_LAST,
                        preferred_element_type=jnp.float32,
                    )
                    new_top = jnp.maximum(top, jnp.max(score, axis=1, keepdims=True))
                    wide_top = jnp.concatenate([new_top] * (size // HEAD_DIM), axis=1)
                    weight = jnp.exp2((score - wide_top) * SCALE)
                    factor = jnp.exp2((top - new_top) * SCALE)
                    total = total * factor + jnp.sum(weight, axis=1, keepdims=True)
                    out = out * factor + jnp.dot(
                        weight.astype(jnp.bfloat16),
                        v_ref[low:, cols],
                        preferred_element_type=jnp.float32,
                    )
                o_all[here, cols] = (out * (1.0 / total)).astype(jnp.bfloat16)
            for d in range(RING):
                copy = pltpu.make_async_copy(o_all.at[here, :], outs[d], sem.at[d])
                pl.when(lax.rem(place + d, RING) == s)(copy.start)
        for d in range(RING):
            pltpu.make_async_copy(o_all.at[:rows, :], outs[d], sem.at[d]).wait()

    return pl.pallas_call(
        kernel,
        out_shape=[jax.ShapeDtypeStruct((rows, part), jnp.bfloat16) for _ in range(RING)],
        in_specs=[SMEM] + [VMEM] * 7,
        out_specs=[VMEM] * RING,
        scratch_shapes=[
            pltpu.VMEM((span, part), jnp.bfloat16),
            pltpu.SemaphoreType.DMA((RING,)),
        ],
        compiler_params=params(20),
        name="attend_halo",
    )(place, begin, *sums, queries, key_halo, value_halo)


def shards(conv_in, norm_gain, filters, gate, queries, keys, doc_lengths):
    rows, width = conv_in.shape
    count = lax.axis_size("seq")
    index = lax.axis_index("seq")
    base = index * rows
    place = lax.rem(index, RING)
    ring_base = (index - place) * rows
    place = place.reshape(1)

    def ring_perm(value, step):
        pairs = [
            (r + i, r + (i + step) % RING) for r in range(0, count, RING) for i in range(RING)
        ]
        return lax.ppermute(value, "seq", pairs)

    def exchange(pieces):
        return [pieces[0]] + [ring_perm(pieces[d], d) for d in range(1, RING)]

    def ahead(value, step):
        return lax.ppermute(value, "seq", [(i, i + step) for i in range(count - step)])

    wide = conv_in.astype(jnp.float32)
    energy = lax.psum(jnp.sum(wide * wide, axis=1), "ch")
    rms = lax.rsqrt(energy / CONV_CH + 1e-06)
    rms_wide = jnp.broadcast_to(rms[:, None], (rows, 128))
    last = (
        conv_in[rows - TAPS :].astype(jnp.float32)
        * rms[rows - TAPS :, None]
        * norm_gain[None, :]
    ).astype(jnp.bfloat16)
    tail = ahead(last, 1)
    query_out, key_out = quarters(place, queries, keys)
    key_in = exchange(key_out)

    positions = ring_base + jnp.arange(rows * RING, dtype=jnp.int32)
    begin_ring = begin_of(doc_lengths, positions)
    begin_att = jnp.broadcast_to(
        (begin_ring - ring_base)[:, None], (rows * RING, 128)
    )
    begin_own = begin_of(doc_lengths, base + jnp.arange(rows, dtype=jnp.int32)) - base
    begin_conv = jnp.broadcast_to(begin_own[:, None], (rows, 128))

    taps = filters[:, ::-1].astype(jnp.float32)
    rest, part, bands = convolve_own(
        place, conv_in, rms_wide, norm_gain[None, :], taps, gate, begin_conv
    )
    mixed, value_out = convolve_tail(place, tail, part, bands, rest, gate)
    key_in, mixed = lax.optimization_barrier((key_in, mixed))
    key_halo = ahead(last_shards(place, key_in, 1)[0], RING)
    value_in = exchange(value_out)
    late = last_shards(place, value_in, CUTS)
    late, query_out = lax.optimization_barrier((late, query_out))
    query_in = exchange(query_out)
    value_halo = ahead(late[0], RING)
    *sums, query_all = attend_ring(place, begin_att, query_in, key_in, value_in)
    pieces = attend_halo(place, begin_att, sums, query_all, key_halo, value_halo)
    attended = whole_width(place, [exchange(pieces)])
    return (mixed, attended)


def solution(mesh):
    placed = (
        P("seq", "ch"),
        P("ch"),
        P("ch", None),
        P("seq", "ch"),
        P("seq", "ch"),
        P("seq", "ch"),
        P(),
    )
    return jax.shard_map(
        shards,
        mesh=mesh,
        in_specs=placed,
        out_specs=(P("seq", "ch"), P("seq", "ch")),
        check_vma=False,
    )
```

```python
import jax
import jax.numpy as jnp
from jax import lax
from jax.experimental import pallas as pl
from jax.experimental.pallas import tpu as pltpu
from jax.sharding import PartitionSpec as P

HEAD_DIM = 128
GROUP = 16
TAPS = 128
CONV_CH = 4096
RING = 4
CUTS = 1
MIB = 1024 * 1024
HBM = pl.BlockSpec(memory_space=pltpu.HBM)
SMEM = pl.BlockSpec(memory_space=pltpu.SMEM)
VMEM = pl.BlockSpec(memory_space=pltpu.VMEM)
NEG = -1e30


def params(mib):
    return pltpu.CompilerParams(vmem_limit_bytes=mib * MIB)


def quarters(place, *arrays):
    rows, width = arrays[0].shape
    part = width // RING
    count = len(arrays)

    def kernel(place_ref, *refs):
        ins, outs, sem = refs[:count], refs[count : count + count * RING], refs[-1]
        place = place_ref[0]
        copies = []
        for a in range(count):
            for d in range(RING):
                low = pl.multiple_of(lax.rem(place + d, RING) * part, part)
                copies.append(
                    pltpu.make_async_copy(
                        ins[a].at[:, pl.ds(low, part)], outs[a * RING + d], sem.at[a * RING + d]
                    )
                )
        for copy in copies:
            copy.start()
        for copy in copies:
            copy.wait()

    out = pl.pallas_call(
        kernel,
        out_shape=[
            jax.ShapeDtypeStruct((rows, part), arrays[0].dtype) for _ in range(count * RING)
        ],
        in_specs=[SMEM] + [HBM] * count,
        out_specs=[VMEM] * (count * RING),
        scratch_shapes=[pltpu.SemaphoreType.DMA((count * RING,))],
        compiler_params=params(8),
        name="quarters",
    )(place, *arrays)
    return [out[a * RING : (a + 1) * RING] for a in range(count)]


def whole_width(place, sets):
    rows, width = sets[0][0].shape
    cuts = len(sets)

    def kernel(place_ref, *refs):
        ins, out, sem = refs[: RING * cuts], refs[RING * cuts], refs[-1]
        place = place_ref[0]
        copies = []
        for c in range(cuts):
            for d in range(RING):
                at = c * RING + d
                low = (lax.rem(place + RING - d, RING) * cuts + c) * width
                cols = pl.ds(pl.multiple_of(low, width), width)
                copies.append(pltpu.make_async_copy(ins[at], out.at[:, cols], sem.at[at]))
        for copy in copies:
            copy.start()
        for copy in copies:
            copy.wait()

    return pl.pallas_call(
        kernel,
        out_shape=jax.ShapeDtypeStruct((rows, width * cuts * RING), sets[0][0].dtype),
        in_specs=[SMEM] + [VMEM] * (RING * cuts),
        out_specs=HBM,
        scratch_shapes=[pltpu.SemaphoreType.DMA((RING * cuts,))],
        compiler_params=params(8),
        name="whole_width",
    )(place, *[piece for pieces in sets for piece in pieces])


def last_shards(place, pieces, cuts):
    rows, part = pieces[0].shape
    width = part // cuts

    def kernel(place_ref, *refs):
        ins, outs, sem = refs[:RING], refs[RING : RING + cuts], refs[-1]
        place = place_ref[0]

        def copy_of(d, c):
            shard = lax.rem(place + RING - d, RING)
            low = pl.multiple_of(jnp.maximum(shard - 1, 0) * rows, rows)
            return shard, pltpu.make_async_copy(
                ins[d].at[:, pl.ds(c * width, width)],
                outs[c].at[pl.ds(low, rows), :],
                sem.at[d * cuts + c],
            )

        every = [(d, c) for d in range(RING) for c in range(cuts)]
        for d, c in every:
            shard, copy = copy_of(d, c)
            pl.when(shard > 0)(copy.start)
        for d, c in every:
            shard, copy = copy_of(d, c)
            pl.when(shard > 0)(copy.wait)

    return pl.pallas_call(
        kernel,
        out_shape=[
            jax.ShapeDtypeStruct((rows * (RING - 1), width), pieces[0].dtype) for _ in range(cuts)
        ],
        in_specs=[SMEM] + [VMEM] * RING,
        out_specs=[VMEM] * cuts,
        scratch_shapes=[pltpu.SemaphoreType.DMA((RING * cuts,))],
        compiler_params=params(8),
        name="last_shards",
    )(place, *pieces)


def lead_in(conv_in, gain):
    rows, width = conv_in.shape
    step = 128
    parts = rows // step

    def kernel(x_hbm, gain_in, x_ref, energy_ref, gain_ref, sem):
        gain_ref[...] = gain_in[...]
        copies = [
            pltpu.make_async_copy(
                x_hbm.at[pl.ds(p * step, step), :], x_ref.at[pl.ds(p * step, step), :], sem.at[p]
            )
            for p in range(parts)
        ]
        for copy in copies:
            copy.start()
        for p in range(parts):
            copies[p].wait()
            here = slice(p * step, (p + 1) * step)
            total = jnp.zeros((step, 128), jnp.float32)
            for at in range(0, width, 128):
                wide = x_ref[here, at : at + 128].astype(jnp.float32)
                total = total + wide * wide
            energy_ref[p : p + 1, :] = jnp.sum(total.T, axis=0, keepdims=True)

    return pl.pallas_call(
        kernel,
        out_shape=[
            jax.ShapeDtypeStruct((rows, width), conv_in.dtype),
            jax.ShapeDtypeStruct((parts, step), jnp.float32),
            jax.ShapeDtypeStruct(gain.shape, jnp.float32),
        ],
        in_specs=[HBM, VMEM],
        out_specs=[VMEM] * 3,
        scratch_shapes=[pltpu.SemaphoreType.DMA((parts,))],
        compiler_params=params(8),
        name="lead_in",
    )(conv_in, gain)


def as_column(line):
    return jnp.broadcast_to(line, (128, 128)).T


def norm_last(conv_in, energy, gain):
    rows, width = conv_in.shape

    def kernel(x_ref, energy_ref, gain_ref, out_ref):
        rms = lax.rsqrt(as_column(energy_ref[rows // 128 - 1 :, :]) / CONV_CH + 1e-06)
        for at in range(0, width, 128):
            cols = slice(at, at + 128)
            out_ref[:, cols] = (
                x_ref[rows - TAPS :, cols].astype(jnp.float32) * rms * gain_ref[:, cols]
            ).astype(jnp.bfloat16)

    return pl.pallas_call(
        kernel,
        out_shape=jax.ShapeDtypeStruct((TAPS, width), jnp.bfloat16),
        in_specs=[VMEM] * 3,
        out_specs=VMEM,
        compiler_params=params(8),
        name="norm_last",
    )(conv_in, energy, gain)


def begin_from(lengths_ref, base, rows):
    position = lax.broadcasted_iota(jnp.int32, (8, 128), 0) * 128
    position = position + lax.broadcasted_iota(jnp.int32, (8, 128), 1)
    begin = jnp.full((8, 128), 0, jnp.int32) - base
    start = 0 - base
    for i in range(lengths_ref.shape[0] - 1):
        start = start + lengths_ref[i]
        begin = jnp.where(position >= start, start, begin)
    return begin.astype(jnp.float32)


def ring_begins(lengths, ring_base, rows):
    def kernel(lengths_ref, base_ref, begin_ref, edge_ref):
        base = base_ref[0]
        lines = begin_from(lengths_ref, base, rows * RING)
        for b in range(rows * RING // 128):
            begin_ref[b * 128 : (b + 1) * 128, :] = as_column(lines[b : b + 1, :]).astype(
                jnp.int32
            )
        for s in range(RING):
            start = 0 - base
            edge = start
            for i in range(lengths_ref.shape[0] - 1):
                start = start + lengths_ref[i]
                edge = jnp.where(start <= s * rows, start, edge)
            edge_ref[s] = edge

    return pl.pallas_call(
        kernel,
        out_shape=[
            jax.ShapeDtypeStruct((rows * RING, 128), jnp.int32),
            jax.ShapeDtypeStruct((RING,), jnp.int32),
        ],
        in_specs=[SMEM] * 2,
        out_specs=[VMEM, SMEM],
        compiler_params=params(8),
        name="ring_begins",
    )(lengths, ring_base)


def convolve_own(base, lengths, conv_in, energy, gain, filters, gate):
    rows, width = conv_in.shape
    lanes = 128
    per = lanes // GROUP
    blocks = rows // TAPS

    def kernel(
        base_ref, lengths_ref, x_ref, energy_ref, gain_ref, filter_ref, gate_ref, *refs
    ):
        mixed_ref, part_ref, band_ref, masks, src, lhs, rms_ref, taps_ref = refs
        for b in range(rows // 128):
            column = as_column(energy_ref[b : b + 1, :])
            rms_ref[b * 128 : (b + 1) * 128, :] = lax.rsqrt(column / CONV_CH + 1e-06)
        begin = begin_from(lengths_ref, base_ref[0], rows)
        out_row = lax.broadcasted_iota(jnp.int32, (TAPS, lanes), 0)
        src_col = lax.broadcasted_iota(jnp.int32, (TAPS, lanes), 1)
        for b in range(blocks):
            first = as_column(begin[b : b + 1, :]).astype(jnp.int32)
            low = b * TAPS
            before = (src_col > out_row) & (src_col + (low - TAPS) >= first)
            inside = (src_col <= out_row) & (src_col + low >= first)
            masks[2 * b] = jnp.where(before, 1.0, 0.0).astype(jnp.bfloat16)
            masks[2 * b + 1] = jnp.where(inside, 1.0, 0.0).astype(jnp.bfloat16)
        lane_group = lax.broadcasted_iota(jnp.int32, (TAPS, lanes), 1) // GROUP
        flip = jnp.where(src_col + out_row == TAPS - 1, 1.0, 0.0).astype(jnp.bfloat16)
        taps_ref[...] = jnp.dot(filter_ref[...], flip, preferred_element_type=jnp.float32)

        def pick(full):
            picked = full[:TAPS]
            for j in range(1, per):
                picked = jnp.where(lane_group == j, full[j * TAPS : (j + 1) * TAPS], picked)
            return picked

        for at in range(width // lanes):
            cols = slice(at * lanes, (at + 1) * lanes)
            src[...] = (
                x_ref[:, cols].astype(jnp.float32) * rms_ref[...] * gain_ref[:, cols]
            ).astype(jnp.bfloat16)
            for j in range(per):
                line = jnp.broadcast_to(
                    taps_ref[at * per + j : at * per + j + 1, :], (TAPS, lanes)
                )
                band = pltpu.roll(line, 1, 1, stride=1, stride_axis=0).astype(jnp.bfloat16)
                spot = slice(j * TAPS, (j + 1) * TAPS)
                band_ref[at, spot, :] = band * masks[0]
                lhs[0, spot, :lanes] = band * masks[1]
                for b in range(1, blocks):
                    lhs[b, spot, :lanes] = band * masks[2 * b]
                    lhs[b, spot, lanes:] = band * masks[2 * b + 1]
            part_ref[:, cols] = pick(
                jnp.dot(lhs[0, :, :lanes], src[:TAPS, :], preferred_element_type=jnp.float32)
            )
            for b in range(1, blocks):
                full = jnp.dot(
                    lhs[b],
                    src[(b - 1) * TAPS : (b + 1) * TAPS, :],
                    preferred_element_type=jnp.float32,
                )
                here = slice(b * TAPS, (b + 1) * TAPS)
                mixed_ref[(b - 1) * TAPS : b * TAPS, cols] = (
                    gate_ref[here, cols].astype(jnp.float32) * pick(full)
                ).astype(jnp.bfloat16)

    return pl.pallas_call(
        kernel,
        out_shape=[
            jax.ShapeDtypeStruct((rows - TAPS, width), jnp.bfloat16),
            jax.ShapeDtypeStruct((TAPS, width), jnp.float32),
            jax.ShapeDtypeStruct((width // lanes, per * TAPS, lanes), jnp.bfloat16),
        ],
        in_specs=[SMEM] * 2 + [VMEM] * 5,
        out_specs=[VMEM] * 3,
        scratch_shapes=[
            pltpu.VMEM((2 * blocks, TAPS, lanes), jnp.bfloat16),
            pltpu.VMEM((rows, lanes), jnp.bfloat16),
            pltpu.VMEM((blocks, per * TAPS, 2 * lanes), jnp.bfloat16),
            pltpu.VMEM((rows, lanes), jnp.float32),
            pltpu.VMEM(filters.shape, jnp.float32),
        ],
        compiler_params=params(20),
        name="convolve_own",
    )(base, lengths, conv_in, energy, gain, filters, gate)


def convolve_tail(place, tail, part, bands, rest, gate):
    width = tail.shape[1]
    rows = TAPS + rest.shape[0]
    block = width // RING
    lanes = 128
    per = lanes // GROUP

    def kernel(place_ref, tail_ref, part_ref, band_ref, rest_ref, gate_ref, *refs):
        mixed_ref, outs = refs[0], refs[1:]
        place = place_ref[0]
        lane_group = lax.broadcasted_iota(jnp.int32, (TAPS, lanes), 1) // GROUP
        for d in range(RING):
            for c in range(block // lanes):
                at = lax.rem(place + d, RING) * (block // lanes) + c
                cols = pl.ds(pl.multiple_of(at * lanes, lanes), lanes)
                mine = slice(c * lanes, (c + 1) * lanes)
                full = jnp.dot(band_ref[at], tail_ref[:, cols], preferred_element_type=jnp.float32)
                picked = full[:TAPS]
                for j in range(1, per):
                    picked = jnp.where(lane_group == j, full[j * TAPS : (j + 1) * TAPS], picked)
                out = (
                    gate_ref[:TAPS, cols].astype(jnp.float32) * (part_ref[:, cols] + picked)
                ).astype(jnp.bfloat16)
                mixed_ref[:TAPS, cols] = out
                outs[d][:TAPS, mine] = out
                other = rest_ref[:, cols]
                mixed_ref[TAPS:, cols] = other
                outs[d][TAPS:, mine] = other

    out = pl.pallas_call(
        kernel,
        out_shape=[jax.ShapeDtypeStruct((rows, width), jnp.bfloat16)]
        + [jax.ShapeDtypeStruct((rows, block), jnp.bfloat16) for _ in range(RING)],
        in_specs=[SMEM] + [VMEM] * 5,
        out_specs=[VMEM] * (1 + RING),
        compiler_params=params(16),
        name="convolve_tail",
    )(place, tail, part, bands, rest, gate)
    return out[0], list(out[1:])


SCALE = HEAD_DIM**-0.5 * 1.4426950408889634
BOTH_LAST = (((1,), (1,)), ((), ()))


def attend_ring(place, begin, queries, keys, values):
    rows, part = queries[0].shape
    heads = part // HEAD_DIM
    span = RING * rows

    def kernel(place_ref, begin_ref, *refs):
        ins = (refs[:RING], refs[RING : 2 * RING], refs[2 * RING : 3 * RING])
        acc_ref, top_ref, total_ref, q_all, k_all, v_all, sem = refs[3 * RING :]
        alls = (q_all, k_all, v_all)
        place = place_ref[0]
        for d in range(RING):
            shard = lax.rem(place + RING - d, RING)
            low = pl.multiple_of(shard * rows, rows)
            for a in range(3):
                pltpu.make_async_copy(
                    ins[a][d], alls[a].at[pl.ds(low, rows), :], sem.at[a, shard]
                ).start()
        for s in range(RING):
            here = slice(s * rows, (s + 1) * rows)
            size = (s + 1) * rows
            for a in range(3):
                pltpu.make_async_copy(ins[a][0], alls[a].at[here, :], sem.at[a, s]).wait()
            first = begin_ref[here, :]
            key = lax.broadcasted_iota(jnp.int32, (rows, 128), 1)
            row = lax.broadcasted_iota(jnp.int32, (rows, 128), 0) + s * rows
            bias = []
            for c in range(size // 128):
                valid = key + c * 128 >= first
                if (c + 1) * 128 > s * rows:
                    valid = valid & (key + c * 128 <= row)
                bias.append(jnp.where(valid, 0.0, NEG))
            bias = jnp.concatenate(bias, axis=1)
            scores = [
                lax.dot_general(
                    q_all[here, h * HEAD_DIM : (h + 1) * HEAD_DIM],
                    k_all[:size, h * HEAD_DIM : (h + 1) * HEAD_DIM],
                    BOTH_LAST,
                    preferred_element_type=jnp.float32,
                )
                for h in range(heads)
            ]
            for h in range(heads):
                cols = slice(h * HEAD_DIM, (h + 1) * HEAD_DIM)
                score = bias + scores[h]
                top = jnp.max(score, axis=1, keepdims=True)
                weight = jnp.exp2((score - top) * SCALE)
                total = jnp.sum(weight, axis=1, keepdims=True)
                acc_ref[here, cols] = jnp.dot(
                    weight.astype(jnp.bfloat16),
                    v_all[:size, cols],
                    preferred_element_type=jnp.float32,
                )
                top_ref[here, cols] = jnp.broadcast_to(top, (rows, HEAD_DIM))
                total_ref[here, cols] = jnp.broadcast_to(total, (rows, HEAD_DIM))

    return pl.pallas_call(
        kernel,
        out_shape=[jax.ShapeDtypeStruct((span, part), jnp.float32) for _ in range(3)]
        + [jax.ShapeDtypeStruct((span, part), jnp.bfloat16)],
        in_specs=[SMEM] + [VMEM] * (1 + 3 * RING),
        out_specs=[VMEM] * 4,
        scratch_shapes=[
            pltpu.VMEM((span, part), jnp.bfloat16),
            pltpu.VMEM((span, part), jnp.bfloat16),
            pltpu.SemaphoreType.DMA((3, RING)),
        ],
        compiler_params=params(20),
        name="attend_ring",
    )(place, begin, *queries, *keys, *values)


def attend_halo(place, edges, begin, sums, queries, key_halo, value_halo):
    back, part = value_halo.shape
    rows = back // (RING - 1)
    heads = part // HEAD_DIM
    span = RING * rows

    def kernel(
        place_ref, edge_ref, begin_ref, acc_ref, top_ref, total_ref, q_ref, k_ref, v_ref, *refs
    ):
        outs, o_all, sem = refs[:RING], refs[RING], refs[RING + 1]
        place = place_ref[0]
        def tile(s, blocks):
            here = slice(s * rows, (s + 1) * rows)
            low = back - blocks * rows
            size = blocks * rows
            if size:
                first = begin_ref[here, :]
                key = lax.broadcasted_iota(jnp.int32, (rows, 128), 1) - size
                bias = jnp.concatenate(
                    [jnp.where(key + c * 128 >= first, 0.0, NEG) for c in range(size // 128)],
                    axis=1,
                )
            scores = []
            for h in range(heads):
                cols = slice(h * HEAD_DIM, (h + 1) * HEAD_DIM)
                if size:
                    scores.append(
                        lax.dot_general(
                            q_ref[here, cols],
                            k_ref[low:, cols],
                            BOTH_LAST,
                            preferred_element_type=jnp.float32,
                        )
                    )
            for h in range(heads):
                cols = slice(h * HEAD_DIM, (h + 1) * HEAD_DIM)
                top = top_ref[here, cols]
                total = total_ref[here, cols]
                out = acc_ref[here, cols]
                if size:
                    score = bias + scores[h]
                    new_top = jnp.maximum(top, jnp.max(score, axis=1, keepdims=True))
                    wide_top = jnp.concatenate([new_top] * (size // HEAD_DIM), axis=1)
                    weight = jnp.exp2((score - wide_top) * SCALE)
                    factor = jnp.exp2((top - new_top) * SCALE)
                    total = total * factor + jnp.sum(weight, axis=1, keepdims=True)
                    out = out * factor + jnp.dot(
                        weight.astype(jnp.bfloat16),
                        v_ref[low:, cols],
                        preferred_element_type=jnp.float32,
                    )
                o_all[here, cols] = (out * (1.0 / total)).astype(jnp.bfloat16)

        for s in (3, 0, 1, 2):
            here = slice(s * rows, (s + 1) * rows)
            most = RING - 1 - s
            if most == 0:
                tile(s, 0)
            need = -edge_ref[s]
            for blocks in range(most + 1 if most else 0):
                above = need > (blocks - 1) * rows
                below = need <= blocks * rows
                if blocks == 0:
                    pl.when(below)(lambda s=s: tile(s, 0))
                elif blocks == most:
                    pl.when(above)(lambda s=s, blocks=blocks: tile(s, blocks))
                else:
                    pl.when(above & below)(lambda s=s, blocks=blocks: tile(s, blocks))
            for d in range(RING):
                copy = pltpu.make_async_copy(o_all.at[here, :], outs[d], sem.at[d])
                pl.when(lax.rem(place + d, RING) == s)(copy.start)
        for d in range(RING):
            pltpu.make_async_copy(o_all.at[:rows, :], outs[d], sem.at[d]).wait()

    return pl.pallas_call(
        kernel,
        out_shape=[jax.ShapeDtypeStruct((rows, part), jnp.bfloat16) for _ in range(RING)],
        in_specs=[SMEM, SMEM] + [VMEM] * 7,
        out_specs=[VMEM] * RING,
        scratch_shapes=[
            pltpu.VMEM((span, part), jnp.bfloat16),
            pltpu.SemaphoreType.DMA((RING,)),
        ],
        compiler_params=params(20),
        name="attend_halo",
    )(place, edges, begin, *sums, queries, key_halo, value_halo)


def shards(conv_in, norm_gain, filters, gate, queries, keys, doc_lengths):
    rows, width = conv_in.shape
    count = lax.axis_size("seq")
    index = lax.axis_index("seq")
    base = index * rows
    place = lax.rem(index, RING)
    ring_base = (index - place) * rows
    place = place.reshape(1)

    def ring_perm(value, step):
        pairs = [
            (r + i, r + (i + step) % RING) for r in range(0, count, RING) for i in range(RING)
        ]
        return lax.ppermute(value, "seq", pairs)

    def exchange(pieces):
        return [pieces[0]] + [ring_perm(pieces[d], d) for d in range(1, RING)]

    def ahead(value, step):
        return lax.ppermute(value, "seq", [(i, i + step) for i in range(count - step)])

    lead, energy, gain = lead_in(conv_in, norm_gain[None, :])
    energy = lax.psum(energy, "ch")
    tail = ahead(norm_last(lead, energy, gain), 1)
    keys, queries, energy = lax.optimization_barrier((keys, queries, energy))
    query_out, key_out = quarters(place, queries, keys)
    key_in = exchange(key_out)

    rest, part, bands = convolve_own(
        base.reshape(1), doc_lengths, lead, energy, gain, filters, gate
    )
    mixed, value_out = convolve_tail(place, tail, part, bands, rest, gate)
    lengths, mixed = lax.optimization_barrier((doc_lengths, mixed))
    begin_att, edges = ring_begins(lengths, ring_base.reshape(1), rows)
    key_in, mixed = lax.optimization_barrier((key_in, mixed))
    key_halo = ahead(last_shards(place, key_in, 1)[0], RING)
    value_in = exchange(value_out)
    late = last_shards(place, value_in, CUTS)
    late, query_out = lax.optimization_barrier((late, query_out))
    query_in = exchange(query_out)
    value_halo = ahead(late[0], RING)
    *sums, query_all = attend_ring(place, begin_att, query_in, key_in, value_in)
    pieces = attend_halo(place, edges, begin_att, sums, query_all, key_halo, value_halo)
    attended = whole_width(place, [exchange(pieces)])
    return (mixed, attended)


def solution(mesh):
    placed = (
        P("seq", "ch"),
        P("ch"),
        P("ch", None),
        P("seq", "ch"),
        P("seq", "ch"),
        P("seq", "ch"),
        P(),
    )
    return jax.shard_map(
        shards,
        mesh=mesh,
        in_specs=placed,
        out_specs=(P("seq", "ch"), P("seq", "ch")),
        check_vma=False,
    )
```
